512 devices in a mesh: rep: 16 (over z, core), fsdp: 32 (over y, x).
Axes of the slice: x: 4, y: 8, z: 8, core: 2. Of those that a mesh axis runs over, the one named last changes fastest.
Arguments:
- parent: bfloat16 [1024, 8192], P('fsdp'), may hold values from -6 to 6
- local_weights: bfloat16 [16, 1024, 8192], P('rep', 'fsdp'), may hold values from -6 to 6
- error: float32 [16, 1024, 8192], P('rep', 'fsdp'), may hold values from -4 to 4
- q_start: bfloat16 [8192, 128], P('fsdp'), may hold values from -0.0625 to 0.0625
Outputs:
- update: bfloat16 [1024, 8192], P('fsdp')
- new_error: float32 [16, 1024, 8192], P('rep', 'fsdp')
- new_q: float32 [8192, 128], P('fsdp')
The draws below stay inside these ranges and needn't reach their ends.
All inputs are finite; a program needn't handle non-finite values.
Results may differ from the reference program's by a relative error of at most 0.022.
Values may be sent and summed in bfloat16 or wider, within the bound.
No kernel may reach another device: no remote copies, remote signals or barrier semaphores. Data moves between devices by JAX's collectives and lax.ppermute only.
A program may use at most 64 MiB of HBM per device.

```python
import jax
import jax.numpy as jnp
from jax import lax

D = 8192
R = 128
ROWS = 1024
N_REP = 16


def steps_of(stream_key, extent, cuts, low, top_value):
    def one(axis_at, shards_of):
        heights = jax.random.uniform(jax.random.fold_in(jax.random.fold_in(stream_key, 6), axis_at), (shards_of,), jnp.float32, low / len(cuts), top_value / len(cuts))
        return jnp.repeat(jnp.exp(heights), extent[axis_at] // shards_of).reshape((-1,) + (1,) * (len(extent) - axis_at - 1))

    factor_of = one(*cuts[0])
    for cut in cuts[1:]:
        factor_of = factor_of * one(*cut)
    return factor_of


def centred(own_key, dims, spread, bound, shards=(), dtype=jnp.bfloat16):
    gain = steps_of(own_key, dims, shards, -0.22, 0.18) if shards else 1.0
    drawn = jax.random.normal(own_key, dims, jnp.float32) * spread * gain
    return jnp.minimum(jnp.maximum(drawn, -bound), bound).astype(dtype)


def setup_inputs(seed: int = 0) -> dict:
    seeds = jax.random.split(jax.random.key(seed), 5)
    parent = centred(seeds[0], (ROWS, D), 1.0, 6.0, ((0, 32),))
    local_weights = centred(seeds[1], (N_REP, ROWS, D), 1.0, 6.0, ((0, 16), (1, 32)))
    error = centred(seeds[2], (N_REP, ROWS, D), 0.5, 4.0, ((0, 16), (1, 32)), jnp.float32)
    q_start = centred(seeds[3], (D, R), D ** -0.5, 0.0625, ((0, 32),))
    return dict(parent=parent, local_weights=local_weights, error=error, q_start=q_start)


def reference(parent, local_weights, error, q_start):
    merged = local_weights.astype(jnp.float32) - parent.astype(jnp.float32)[None] + error
    merged_bf = merged.astype(jnp.bfloat16)
    merged_wide = merged_bf.astype(jnp.float32)
    p_each = jnp.einsum('rnd,dk->rnk', merged_wide, q_start.astype(jnp.float32))
    mean_p = jnp.sum(p_each, axis=0) / N_REP
    gram = jnp.dot(mean_p.T, mean_p, precision=lax.Precision.HIGHEST)
    lower = jnp.linalg.cholesky(gram)
    ortho = jax.scipy.linalg.solve_triangular(lower, mean_p.T, lower=True).T
    ortho_bf = ortho.astype(jnp.bfloat16)
    q_sum = jnp.einsum('rnd,nk->dk', merged_wide, ortho_bf.astype(jnp.float32))
    new_q = q_sum / N_REP
    approx = jnp.dot(ortho_bf.astype(jnp.float32), new_q.astype(jnp.bfloat16).T.astype(jnp.float32), preferred_element_type=jnp.float32)
    return (approx.astype(jnp.bfloat16), merged - approx[None], new_q)
```

```python
import jax
import jax.numpy as jnp
from jax import lax
from jax.experimental import pallas as pl
from jax.experimental.pallas import tpu as pltpu
from jax.sharding import PartitionSpec as P

HIGHEST = lax.Precision.HIGHEST
F32 = jnp.float32
BF16 = jnp.bfloat16
D, R, NREP, NF = 8192, 128, 16, 32
NX, NY, NZ = 4, 8, 8
ROWS = 32
COLS = D // NREP
QROWS = D // NF
VMEM = pl.BlockSpec(memory_space=pltpu.VMEM)
SMEM = pl.BlockSpec(memory_space=pltpu.SMEM)
LIGHT = pl.CostEstimate(flops=1, bytes_accessed=1, transcendentals=0)
WIDE = pltpu.CompilerParams(vmem_limit_bytes=60 * 1024 * 1024)
PARAMS = pltpu.CompilerParams(vmem_limit_bytes=32 * 1024 * 1024)


def dot(a, b, dims):
    return lax.dot_general(a, b, (dims, ((), ())), precision=HIGHEST, preferred_element_type=F32)


def transpose_groups(tiles):
    group = lax.broadcasted_iota(jnp.int32, tiles[0].shape, 1) // 16
    tiles = list(tiles)
    for step in (1, 2, 4):
        upper = (group & step) != 0
        for i in range(8):
            if i & step:
                continue
            x, y = tiles[i], tiles[i + step]
            tiles[i] = jnp.where(upper, pltpu.roll(y, 16 * step, 1), x)
            tiles[i + step] = jnp.where(upper, y, pltpu.roll(x, 128 - 16 * step, 1))
    return tiles


def tile_at(i, h):
    return slice(128 * (2 * i + h), 128 * (2 * i + h) + 128)


def share_kernel(place, q, out, sems):
    mine = q.at[pl.ds(pl.multiple_of(16 * place[0], 16), 16), :]
    copies = [pltpu.make_async_copy(mine, out.at[y], sems.at[y]) for y in range(NY)]
    for copy in copies:
        copy.start()
    for copy in copies:
        copy.wait()


def share(place, q):
    return pl.pallas_call(
        share_kernel,
        out_shape=jax.ShapeDtypeStruct((NY, 16, R), BF16),
        in_specs=[SMEM, pl.BlockSpec(memory_space=pltpu.HBM)],
        out_specs=VMEM,
        scratch_shapes=[pltpu.SemaphoreType.DMA((NY,))],
        compiler_params=WIDE,
        name="share",
    )(place, q)


def merge_kernel(parent, local, error, out, parent_v, local_v, error_v, sems):
    def copies(v):
        at = pl.ds(16 * v, 16)
        return [
            pltpu.make_async_copy(error.at[0, at, :], error_v.at[at, :], sems.at[2, v]),
            pltpu.make_async_copy(local.at[0, at, :], local_v.at[at, :], sems.at[1, v]),
            pltpu.make_async_copy(parent.at[at, :], parent_v.at[at, :], sems.at[0, v]),
        ]

    for v in range(2):
        for copy in copies(v):
            copy.start()
    for v in range(2):
        for copy in copies(v):
            copy.wait()
        rows = slice(16 * v, 16 * v + 16)
        for u in range(4):
            for h in range(2):
                tiles = []
                for i in range(8):
                    at = tile_at(8 * u + i, h)
                    merged = local_v[rows, at].astype(F32) - parent_v[rows, at].astype(F32) + error_v[rows, at]
                    tiles.append(merged.astype(BF16))
                for g, tile in enumerate(transpose_groups(tiles)):
                    out[2 * g + h, rows, 128 * u:128 * u + 128] = tile


def merge(parent, local, error):
    hbm = pl.BlockSpec(memory_space=pltpu.HBM)
    return pl.pallas_call(
        merge_kernel,
        out_shape=jax.ShapeDtypeStruct((NREP, ROWS, COLS), BF16),
        in_specs=[hbm, hbm, hbm],
        out_specs=VMEM,
        scratch_shapes=[pltpu.VMEM((ROWS, D), BF16), pltpu.VMEM((ROWS, D), BF16),
                        pltpu.VMEM((ROWS, D), F32), pltpu.SemaphoreType.DMA((3, 2))],
        compiler_params=WIDE,
        cost_estimate=LIGHT, name="merge",
    )(parent, local, error)


def left_kernel(got, q, s_out, p_out):
    s = got[0].astype(F32)
    for r in range(1, NREP):
        s = s + got[r].astype(F32)
    s_out[...] = s
    shares = [q[x, y] for y in range(NY) for x in range(NX)]
    p = dot(s, jnp.concatenate(shares, axis=0).astype(F32), ((1,), (0,)))
    for r in range(NREP):
        p_out[r] = p


def left(got, q):
    return pl.pallas_call(
        left_kernel,
        out_shape=(jax.ShapeDtypeStruct((ROWS, COLS), F32),
                   jax.ShapeDtypeStruct((NREP, ROWS, R), F32)),
        in_specs=[VMEM, VMEM], out_specs=(VMEM, VMEM), compiler_params=PARAMS, name="left",
    )(got, q)


def rows_kernel(parts, s, mean_out, z_out):
    p = parts[0]
    for r in range(1, NREP):
        p = p + parts[r]
    mean = p / NREP
    mean_out[...] = mean
    y = dot(s[...], mean, ((0,), (0,)))
    gram = dot(mean, mean, ((0,), (0,)))
    for f in range(NF):
        for b in range(4):
            z_out[f, :, 128 * b:128 * b + 128] = y[16 * f + 4 * b:16 * f + 4 * b + 4]
        z_out[f, :, COLS:] = gram[4 * f:4 * f + 4]


def rows(parts, s):
    return pl.pallas_call(
        rows_kernel,
        out_shape=(jax.ShapeDtypeStruct((ROWS, R), F32), jax.ShapeDtypeStruct((NF, 4, COLS + R), F32)),
        in_specs=[VMEM, VMEM], out_specs=(VMEM, VMEM), compiler_params=PARAMS, name="rows",
    )(parts, s)


def total_kernel(parts, out):
    t = parts[0]
    for i in range(1, parts.shape[0]):
        t = t + parts[i]
    for i in range(out.shape[0]):
        out[i] = t


def total(parts, copies):
    return pl.pallas_call(
        total_kernel,
        out_shape=jax.ShapeDtypeStruct((copies,) + parts.shape[1:], F32),
        in_specs=[VMEM], out_specs=VMEM, compiler_params=PARAMS, name="total",
    )(parts)


def square(p, x):
    wide = jnp.concatenate([p, x], axis=1)
    high = wide.astype(BF16).astype(F32)
    rest = wide - high
    mid = rest.astype(BF16).astype(F32)
    low = rest - mid
    a = jnp.concatenate([high, high, mid, high, low, mid], axis=0)[:, :R].astype(BF16)
    b = jnp.concatenate([high, mid, high, low, high, mid], axis=0).astype(BF16)
    return lax.dot_general(a, b, (((0,), (0,)), ((), ())), preferred_element_type=F32)


def inverse_factor(gram):
    def spread(x):
        return jnp.broadcast_to(x, (8, R))

    row = lax.broadcasted_iota(jnp.int32, (R, R), 0)
    col = lax.broadcasted_iota(jnp.int32, (R, R), 1)
    unit = (row == col).astype(F32)
    sub = lax.broadcasted_iota(jnp.int32, (8, R), 0)
    count = R // 8
    left = [gram[8 * g:8 * g + 8] for g in range(count)]
    right = [unit[8 * g:8 * g + 8] for g in range(count)]
    for k in range(count):
        last = k == count - 1
        p, x = left[k], right[k]
        d = [spread(p[:, 8 * k + j:8 * k + j + 1]) for j in range(8)]
        if not last:
            n, y = left[k + 1], right[k + 1]
            c = [spread(n[:, 8 * k + j:8 * k + j + 1]) for j in range(8)]
        e = {(i, j): spread(d[j][i:i + 1]) for j in range(8) for i in range(j, 8)}
        for j in range(8):
            inv = lax.rsqrt(e[j, j])
            low = {i: e[i, j] * inv for i in range(j + 1, 8)}
            for m in range(j + 1, 8):
                for i in range(m, 8):
                    e[i, m] = e[i, m] - low[i] * low[m]
            p_row, x_row = spread(p[j:j + 1]) * inv, spread(x[j:j + 1]) * inv
            if j < 7:
                here = jnp.where(sub > j, d[j] * inv, 0.0)
                for m in range(j + 1, 8):
                    d[m] = d[m] - here * low[m]
                p, x = p - here * p_row, x - here * x_row
            p, x = jnp.where(sub == j, p_row, p), jnp.where(sub == j, x_row, x)
            if not last:
                below = c[j] * inv
                for m in range(j + 1, 8):
                    c[m] = c[m] - below * low[m]
                n, y = n - below * p_row, y - below * x_row
        right[k] = x
        if not last:
            left[k + 1], right[k + 1] = n, y
        if k < count - 2:
            update = square(p, x)
            for g in range(k + 2, count):
                left[g] = left[g] - update[8 * g:8 * g + 8, :R]
                right[g] = right[g] - update[8 * g:8 * g + 8, R:]
    return jnp.concatenate(right, axis=0)


def solve_kernel(shard, sums, mean, out, gram, y, q_all):
    for f in range(NF):
        gram[4 * f:4 * f + 4, :] = sums[f, :, COLS:]
        for b in range(4):
            y[16 * f + 4 * b:16 * f + 4 * b + 4, :] = sums[f, :, 128 * b:128 * b + 128]
    linv = inverse_factor(gram[...])
    ortho = dot(mean[...], linv, ((1,), (1,))).astype(BF16)
    q = dot(y[...], linv, ((1,), (1,))) / NREP
    q_all[...] = q
    approx = lax.dot_general(
        ortho, q.astype(BF16), (((1,), (1,)), ((), ())), preferred_element_type=F32).astype(BF16)
    own = q_all[pl.ds(pl.multiple_of(16 * shard[0], 16), 16), :]
    high = own.astype(BF16)
    low = (own - high.astype(F32)).astype(BF16)
    for z in range(NZ):
        out[z, :, :COLS] = approx
        out[z, :16, COLS:] = high
        out[z, 16:, COLS:] = low


def solve(shard, sums, mean):
    return pl.pallas_call(
        solve_kernel,
        out_shape=jax.ShapeDtypeStruct((NZ, ROWS, COLS + R), BF16),
        in_specs=[SMEM, VMEM, VMEM],
        out_specs=VMEM,
        scratch_shapes=[pltpu.VMEM((R, R), F32), pltpu.VMEM((COLS, R), F32), pltpu.VMEM((COLS, R), F32)],
        compiler_params=PARAMS,
        name="solve",
    )(shard, sums, mean)


def finish_kernel(core, parent, local, error, mine, other, update, new_error, new_q,
                  update_v, error_v, q_v, sems):
    copies = []

    def send(source, target):
        copies.append(pltpu.make_async_copy(source, target, sems.at[len(copies)]))
        copies[-1].start()

    parts = (mine, core[0]), (other, 1 - core[0])
    for got, sender in parts:
        for z in range(NZ):
            part = got[z, :, COLS:].astype(F32)
            at = pl.ds(pl.multiple_of(16 * z + QROWS // 2 * sender, 16), 16)
            q_v[at, :] = part[:16] + part[16:]
    send(q_v, new_q)
    for u in range(4):
        for got, sender in parts:
            tiles = transpose_groups([got[z, :, 128 * u:128 * u + 128] for z in range(NZ)])
            for i, approx in enumerate(tiles):
                at = pl.ds(pl.multiple_of(256 * (8 * u + i) + 128 * sender, 128), 128)
                merged = local[0, :, at].astype(F32) - parent[:, at].astype(F32) + error[0, :, at]
                update_v[:, at] = approx
                error_v[:, at] = merged - approx.astype(F32)
        at = pl.ds(u * (D // 4), D // 4)
        send(update_v.at[:, at], update.at[:, at])
        send(error_v.at[:, at], new_error.at[0, :, at])
    for copy in copies:
        copy.wait()


def finish(core, parent, local, error, mine, other):
    hbm = pl.BlockSpec(memory_space=pltpu.HBM)
    return pl.pallas_call(
        finish_kernel,
        out_shape=(jax.ShapeDtypeStruct((ROWS, D), BF16), jax.ShapeDtypeStruct((1, ROWS, D), F32),
                   jax.ShapeDtypeStruct((QROWS, R), F32)),
        in_specs=[SMEM, VMEM, VMEM, VMEM, VMEM, VMEM],
        out_specs=(hbm, hbm, hbm),
        scratch_shapes=[pltpu.VMEM((ROWS, D), BF16), pltpu.VMEM((ROWS, D), F32),
                        pltpu.VMEM((QROWS, R), F32), pltpu.SemaphoreType.DMA((9,))],
        compiler_params=PARAMS,
        name="finish",
    )(core, parent, local, error, mine, other)


def exchange(x, axis):
    return lax.all_to_all(x, axis, 0, 0, tiled=True)


def swap(x):
    return lax.ppermute(x, "core", [(0, 1), (1, 0)])


def per_device(parent, local_weights, error, q_start):
    rep, fsdp = ("z", "core"), ("y", "x")
    core, f = (lax.axis_index(axis) for axis in ("core", fsdp))
    r = lax.axis_index(("core", "z"))
    q = exchange(share(r[None], q_start), "y")
    merged, q = lax.optimization_barrier((merge(parent, local_weights, error), q))
    q = lax.all_gather(q, "x")
    s, p = left(exchange(merged, rep), q)
    mean, z = rows(exchange(p, rep), s)
    z = exchange(total(exchange(z, fsdp), NF), fsdp)
    got = exchange(solve(f[None], z, mean), "z")
    return finish(core[None], parent, local_weights, error, got, swap(got))


def solution(mesh):
    mesh = jax.sharding.Mesh(mesh.devices.reshape(8, 2, 8, 4), ("z", "core", "y", "x"))
    rep, fsdp = ("z", "core"), ("y", "x")
    placed = (P(fsdp, None), P(rep, fsdp, None), P(rep, fsdp, None), P(fsdp, None))
    return jax.shard_map(
        per_device,
        mesh=mesh,
        in_specs=placed,
        out_specs=(P(fsdp, None), P(rep, fsdp, None), P(fsdp, None)),
        check_vma=False,
    )
```

```python
import jax
import jax.numpy as jnp
from jax import lax
from jax.experimental import pallas as pl
from jax.experimental.pallas import tpu as pltpu
from jax.sharding import PartitionSpec as P

HIGHEST = lax.Precision.HIGHEST
F32 = jnp.float32
BF16 = jnp.bfloat16
D, R, NREP, NF = 8192, 128, 16, 32
NX, NY, NZ = 4, 8, 8
ROWS = 32
COLS = D // NREP
QROWS = D // NF
VMEM = pl.BlockSpec(memory_space=pltpu.VMEM)
SMEM = pl.BlockSpec(memory_space=pltpu.SMEM)
LIGHT = pl.CostEstimate(flops=1, bytes_accessed=1, transcendentals=0)
WIDE = pltpu.CompilerParams(vmem_limit_bytes=60 * 1024 * 1024)
PARAMS = pltpu.CompilerParams(vmem_limit_bytes=32 * 1024 * 1024)


def dot(a, b, dims):
    return lax.dot_general(a, b, (dims, ((), ())), precision=HIGHEST, preferred_element_type=F32)


def transpose_groups(tiles):
    group = lax.broadcasted_iota(jnp.int32, tiles[0].shape, 1) // 16
    tiles = list(tiles)
    for step in (1, 2, 4):
        upper = (group & step) != 0
        for i in range(8):
            if i & step:
                continue
            x, y = tiles[i], tiles[i + step]
            tiles[i] = jnp.where(upper, pltpu.roll(y, 16 * step, 1), x)
            tiles[i + step] = jnp.where(upper, y, pltpu.roll(x, 128 - 16 * step, 1))
    return tiles


def tile_at(i, h):
    return slice(128 * (2 * i + h), 128 * (2 * i + h) + 128)


def thirds(x):
    high = x.astype(BF16).astype(F32)
    mid = (x - high).astype(BF16).astype(F32)
    return high, mid, x - high - mid


def cross(a, b):
    (ah, am, al), (bh, bm, bl) = thirds(a), thirds(b)
    a = jnp.concatenate([ah, ah, am, ah, al, am], axis=0).astype(BF16)
    b = jnp.concatenate([bh, bm, bh, bl, bh, bm], axis=0).astype(BF16)
    return lax.dot_general(a, b, (((0,), (0,)), ((), ())), preferred_element_type=F32)


def share_kernel(place, q, out, sems):
    mine = q.at[pl.ds(pl.multiple_of(16 * place[0], 16), 16), :]
    copies = [pltpu.make_async_copy(mine, out.at[y], sems.at[y]) for y in range(NY)]
    for copy in copies:
        copy.start()
    for copy in copies:
        copy.wait()


def share(place, q):
    return pl.pallas_call(
        share_kernel,
        out_shape=jax.ShapeDtypeStruct((NY, 16, R), BF16),
        in_specs=[SMEM, pl.BlockSpec(memory_space=pltpu.HBM)],
        out_specs=VMEM,
        scratch_shapes=[pltpu.SemaphoreType.DMA((NY,))],
        compiler_params=WIDE,
        name="share",
    )(place, q)


def merge_kernel(parent, local, error, out, parent_v, local_v, error_v, sems):
    def copies(v):
        at = pl.ds(16 * v, 16)
        return [
            pltpu.make_async_copy(error.at[0, at, :], error_v.at[at, :], sems.at[2, v]),
            pltpu.make_async_copy(local.at[0, at, :], local_v.at[at, :], sems.at[1, v]),
            pltpu.make_async_copy(parent.at[at, :], parent_v.at[at, :], sems.at[0, v]),
        ]

    for v in range(2):
        for copy in copies(v):
            copy.start()
    for v in range(2):
        for copy in copies(v):
            copy.wait()
        rows = slice(16 * v, 16 * v + 16)
        for u in range(4):
            for h in range(2):
                tiles = []
                for i in range(8):
                    at = tile_at(8 * u + i, h)
                    merged = local_v[rows, at].astype(F32) - parent_v[rows, at].astype(F32) + error_v[rows, at]
                    tiles.append(merged.astype(BF16))
                for g, tile in enumerate(transpose_groups(tiles)):
                    out[2 * g + h, rows, 128 * u:128 * u + 128] = tile


def merge(parent, local, error):
    hbm = pl.BlockSpec(memory_space=pltpu.HBM)
    return pl.pallas_call(
        merge_kernel,
        out_shape=jax.ShapeDtypeStruct((NREP, ROWS, COLS), BF16),
        in_specs=[hbm, hbm, hbm],
        out_specs=VMEM,
        scratch_shapes=[pltpu.VMEM((ROWS, D), BF16), pltpu.VMEM((ROWS, D), BF16),
                        pltpu.VMEM((ROWS, D), F32), pltpu.SemaphoreType.DMA((3, 2))],
        compiler_params=WIDE,
        cost_estimate=LIGHT, name="merge",
    )(parent, local, error)


def left_kernel(got, q, s_out, p_out):
    s = got[0].astype(F32)
    for r in range(1, NREP):
        s = s + got[r].astype(F32)
    s_out[...] = s
    shares = [q[x, y] for y in range(NY) for x in range(NX)]
    q_all = jnp.concatenate(shares, axis=0)
    p = sum(jnp.dot(part.astype(BF16), q_all, preferred_element_type=F32) for part in thirds(s))
    for r in range(NREP):
        p_out[r] = p


def left(got, q):
    return pl.pallas_call(
        left_kernel,
        out_shape=(jax.ShapeDtypeStruct((ROWS, COLS), F32),
                   jax.ShapeDtypeStruct((NREP, ROWS, R), F32)),
        in_specs=[VMEM, VMEM], out_specs=(VMEM, VMEM), compiler_params=PARAMS, name="left",
    )(got, q)


def rows_kernel(parts, s, mean_out, z_out):
    p = parts[0]
    for r in range(1, NREP):
        p = p + parts[r]
    mean = p / NREP
    mean_out[...] = mean
    y = cross(s[...], mean)
    gram = cross(mean, mean)
    for f in range(NF):
        for b in range(4):
            z_out[f, :, 128 * b:128 * b + 128] = y[16 * f + 4 * b:16 * f + 4 * b + 4]
        z_out[f, :, COLS:] = gram[4 * f:4 * f + 4]


def rows(parts, s):
    return pl.pallas_call(
        rows_kernel,
        out_shape=(jax.ShapeDtypeStruct((ROWS, R), F32), jax.ShapeDtypeStruct((NF, 4, COLS + R), F32)),
        in_specs=[VMEM, VMEM], out_specs=(VMEM, VMEM), compiler_params=PARAMS, name="rows",
    )(parts, s)


def total_kernel(parts, out):
    t = parts[0]
    for i in range(1, parts.shape[0]):
        t = t + parts[i]
    for i in range(out.shape[0]):
        out[i] = t


def total(parts, copies):
    return pl.pallas_call(
        total_kernel,
        out_shape=jax.ShapeDtypeStruct((copies,) + parts.shape[1:], F32),
        in_specs=[VMEM], out_specs=VMEM, compiler_params=PARAMS, name="total",
    )(parts)


def inverse_factor(gram):
    def spread(x):
        return jnp.broadcast_to(x, (8, R))

    row = lax.broadcasted_iota(jnp.int32, (R, R), 0)
    col = lax.broadcasted_iota(jnp.int32, (R, R), 1)
    unit = (row == col).astype(F32)
    sub = lax.broadcasted_iota(jnp.int32, (8, R), 0)
    count = R // 8
    left = [gram[8 * g:8 * g + 8] for g in range(count)]
    right = [unit[8 * g:8 * g + 8] for g in range(count)]
    for k in range(count):
        last = k == count - 1
        p, x = left[k], right[k]
        d = [spread(p[:, 8 * k + j:8 * k + j + 1]) for j in range(8)]
        if not last:
            n, y = left[k + 1], right[k + 1]
            c = [spread(n[:, 8 * k + j:8 * k + j + 1]) for j in range(8)]
        e = {(i, j): spread(d[j][i:i + 1]) for j in range(8) for i in range(j, 8)}
        for j in range(8):
            inv = lax.rsqrt(e[j, j])
            low = {i: e[i, j] * inv for i in range(j + 1, 8)}
            for m in range(j + 1, 8):
                for i in range(m, 8):
                    e[i, m] = e[i, m] - low[i] * low[m]
            p_row, x_row = spread(p[j:j + 1]) * inv, spread(x[j:j + 1]) * inv
            if j < 7:
                here = jnp.where(sub > j, d[j] * inv, 0.0)
                for m in range(j + 1, 8):
                    d[m] = d[m] - here * low[m]
                p, x = p - here * p_row, x - here * x_row
            p, x = jnp.where(sub == j, p_row, p), jnp.where(sub == j, x_row, x)
            if not last:
                below = c[j] * inv
                for m in range(j + 1, 8):
                    c[m] = c[m] - below * low[m]
                n, y = n - below * p_row, y - below * x_row
        right[k] = x
        if not last:
            left[k + 1], right[k + 1] = n, y
        if k < count - 2:
            update = cross(p, jnp.concatenate([p, x], axis=1))
            for g in range(k + 2, count):
                left[g] = left[g] - update[8 * g:8 * g + 8, :R]
                right[g] = right[g] - update[8 * g:8 * g + 8, R:]
    return jnp.concatenate(right, axis=0)


def solve_kernel(shard, sums, mean, out, gram, y, q_all):
    for f in range(NF):
        gram[4 * f:4 * f + 4, :] = sums[f, :, COLS:]
        for b in range(4):
            y[16 * f + 4 * b:16 * f + 4 * b + 4, :] = sums[f, :, 128 * b:128 * b + 128]
    linv = inverse_factor(gram[...])
    ortho = dot(mean[...], linv, ((1,), (1,))).astype(BF16)
    q = dot(y[...], linv, ((1,), (1,))) / NREP
    q_all[...] = q
    approx = lax.dot_general(
        ortho, q.astype(BF16), (((1,), (1,)), ((), ())), preferred_element_type=F32).astype(BF16)
    own = q_all[pl.ds(pl.multiple_of(16 * shard[0], 16), 16), :]
    high = own.astype(BF16)
    low = (own - high.astype(F32)).astype(BF16)
    for z in range(NZ):
        out[z, :, :COLS] = approx
        out[z, :16, COLS:] = high
        out[z, 16:, COLS:] = low


def solve(shard, sums, mean):
    return pl.pallas_call(
        solve_kernel,
        out_shape=jax.ShapeDtypeStruct((NZ, ROWS, COLS + R), BF16),
        in_specs=[SMEM, VMEM, VMEM],
        out_specs=VMEM,
        scratch_shapes=[pltpu.VMEM((R, R), F32), pltpu.VMEM((COLS, R), F32), pltpu.VMEM((COLS, R), F32)],
        compiler_params=PARAMS,
        name="solve",
    )(shard, sums, mean)


def finish_kernel(core, parent, local, error, mine, other, update, new_error, new_q,
                  update_v, error_v, q_v, sems):
    copies = []

    def send(source, target):
        copies.append(pltpu.make_async_copy(source, target, sems.at[len(copies)]))
        copies[-1].start()

    parts = (mine, core[0]), (other, 1 - core[0])
    for got, sender in parts:
        for z in range(NZ):
            part = got[z, :, COLS:].astype(F32)
            at = pl.ds(pl.multiple_of(16 * z + QROWS // 2 * sender, 16), 16)
            q_v[at, :] = part[:16] + part[16:]
    send(q_v, new_q)
    for u in range(4):
        for got, sender in parts:
            tiles = transpose_groups([got[z, :, 128 * u:128 * u + 128] for z in range(NZ)])
            for i, approx in enumerate(tiles):
                at = pl.ds(pl.multiple_of(256 * (8 * u + i) + 128 * sender, 128), 128)
                merged = local[0, :, at].astype(F32) - parent[:, at].astype(F32) + error[0, :, at]
                update_v[:, at] = approx
                error_v[:, at] = merged - approx.astype(F32)
        at = pl.ds(u * (D // 4), D // 4)
        send(update_v.at[:, at], update.at[:, at])
        send(error_v.at[:, at], new_error.at[0, :, at])
    for copy in copies:
        copy.wait()


def finish(core, parent, local, error, mine, other):
    hbm = pl.BlockSpec(memory_space=pltpu.HBM)
    return pl.pallas_call(
        finish_kernel,
        out_shape=(jax.ShapeDtypeStruct((ROWS, D), BF16), jax.ShapeDtypeStruct((1, ROWS, D), F32),
                   jax.ShapeDtypeStruct((QROWS, R), F32)),
        in_specs=[SMEM, VMEM, VMEM, VMEM, VMEM, VMEM],
        out_specs=(hbm, hbm, hbm),
        scratch_shapes=[pltpu.VMEM((ROWS, D), BF16), pltpu.VMEM((ROWS, D), F32),
                        pltpu.VMEM((QROWS, R), F32), pltpu.SemaphoreType.DMA((9,))],
        compiler_params=PARAMS,
        name="finish",
    )(core, parent, local, error, mine, other)


def exchange(x, axis):
    return lax.all_to_all(x, axis, 0, 0, tiled=True)


def swap(x):
    return lax.ppermute(x, "core", [(0, 1), (1, 0)])


def per_device(parent, local_weights, error, q_start):
    rep, fsdp = ("z", "core"), ("y", "x")
    core, f = (lax.axis_index(axis) for axis in ("core", fsdp))
    r = lax.axis_index(("core", "z"))
    q = exchange(share(r[None], q_start), "y")
    merged, q = lax.optimization_barrier((merge(parent, local_weights, error), q))
    q = lax.all_gather(q, "x")
    s, p = left(exchange(merged, rep), q)
    mean, z = rows(exchange(p, rep), s)
    z = exchange(total(exchange(z, fsdp), NF), fsdp)
    got = exchange(solve(f[None], z, mean), "z")
    return finish(core[None], parent, local_weights, error, got, swap(got))


def solution(mesh):
    mesh = jax.sharding.Mesh(mesh.devices.reshape(8, 2, 8, 4), ("z", "core", "y", "x"))
    rep, fsdp = ("z", "core"), ("y", "x")
    placed = (P(fsdp, None), P(rep, fsdp, None), P(rep, fsdp, None), P(fsdp, None))
    return jax.shard_map(
        per_device,
        mesh=mesh,
        in_specs=placed,
        out_specs=(P(fsdp, None), P(rep, fsdp, None), P(fsdp, None)),
        check_vma=False,
    )
```
